256 devices in a mesh: pre: 4 (over x_lo, core), main: 64 (over z, x_hi, y).
Axes of the slice: x: 4 (x_hi: 2, x_lo: 2; x = x_hi * 2 + x_lo), y: 4, z: 8, core: 2. Of those that a mesh axis runs over, the one named last changes fastest.
Arguments:
- pre_velocity: float32 [3, 16, 512, 512], P(None, None, 'main', 'pre'), may hold values from -4 to 4
- deck_velocity: float32 [3, 16, 1024, 512], P(None, None, 'main', 'pre'), may hold values from -4 to 4
- deck_force: float32 [16, 1024, 512], P(None, 'main', 'pre'), may hold values from -4 to 4
- inlet_shift: int32 [4], replicated, may hold values from 0 to 511, as said below
- tap_offset: int32 [1024, 4], P('main'), may hold values from -1 to 2
- tap_weight: float32 [1024, 4], P('main'), may hold values from 0.1 to 0.5
- phase_index: int32 [4], replicated, may hold values from 0 to 63
Outputs:
- pre_final: float32 [3, 16, 512, 512], P(None, None, 'main', 'pre')
- deck_final: float32 [3, 16, 1024, 512], P(None, None, 'main', 'pre')
The draws below stay inside these ranges and needn't reach their ends.
Inputs may be any that keep to these rules, and one draw needn't show every extreme that they name: `inlet_shift`: the shifts of the 4 steps include 0, 256 and 511.
All inputs are finite; a program needn't handle non-finite values.
Results may differ from the reference program's by a relative error of at most 0.00005.
Values sent between devices are 32-bit elements; how exact they have to be, the bound alone decides.
A program may use at most 128 MiB of HBM per device.

```python
import jax
import jax.numpy as jnp

PX = 16
MX = 16
STEPS = 4
SWEEPS = 7
TAPS = 4
PERIOD = 64
NYP = 512
NYM = 1024
NZ = 512


def draw_inlet_shift(key, part):
    key = jax.random.fold_in(key, 11)
    first, second = jax.random.split(key)
    values = jax.random.randint(first, (STEPS,), 0, NYP, dtype=jnp.int32)
    values = values.at[0].set(0).at[1].set(NYP - 1).at[2].set(NYP // 2)
    order = jax.random.permutation(second, STEPS)
    return values[order].astype(jnp.int32)


def plant(values, rng, low, largest):
    extent = values.shape
    place = [jax.random.randint(jax.random.fold_in(rng, axis), (), 0, extent[axis]) for axis in range(len(extent))]
    values = values.at[tuple(place)].set(low)
    longest = extent.index(max(extent))
    place[longest] = (place[longest] + 1) % extent[longest]
    return values.at[tuple(place)].set(largest)


def shard_levels(key, shape, cuts, least, high):
    gain = 1.0
    for dim, shards_of in cuts:
        heights = jax.random.uniform(jax.random.fold_in(jax.random.fold_in(key, 6), dim), (shards_of,), jnp.float32, least / len(cuts), high / len(cuts))
        gain = gain * jnp.repeat(jnp.exp(heights), shape[dim] // shards_of).reshape((-1,) + (1,) * (len(shape) - 1 - dim))
    return gain


def bell_draw(stream_key, shape, scale, limit, cuts=(), kind=jnp.bfloat16):
    values = scale * jax.random.normal(stream_key, shape, jnp.float32)
    if cuts:
        values = values * shard_levels(stream_key, shape, cuts, -0.22, 0.18)
    return jnp.clip(values, -limit, limit).astype(kind)


def setup_inputs(seed: int = 0) -> dict:
    arg_keys = jax.random.split(jax.random.key(seed), 8)
    return {
        "pre_velocity": bell_draw(arg_keys[0], (3, PX, NYP, NZ), 1.0, 4.0, ((2, 64), (3, 4)), jnp.float32),
        "deck_velocity": bell_draw(arg_keys[1], (3, MX, NYM, NZ), 1.0, 4.0, ((2, 64), (3, 4)), jnp.float32),
        "deck_force": bell_draw(arg_keys[2], (MX, NYM, NZ), 1.0, 4.0, ((1, 64), (2, 4)), jnp.float32),
        "inlet_shift": draw_inlet_shift(jax.random.fold_in(arg_keys[7], 71), 0),
        "tap_offset": plant(jax.random.randint(arg_keys[4], (NYM, TAPS), -1, 3), jax.random.fold_in(arg_keys[4], 1), -1, 2).astype(jnp.int32),
        "tap_weight": jnp.clip(0.1 + 0.4 * jax.random.uniform(arg_keys[5], (NYM, TAPS), jnp.float32) ** shard_levels(arg_keys[5], (NYM, TAPS), ((0, 64),), -0.2, 0.2), 0.1, 0.5),
        "phase_index": plant(jax.random.randint(arg_keys[6], (STEPS,), 0, PERIOD), jax.random.fold_in(arg_keys[6], 1), 0, PERIOD - 1).astype(jnp.int32),
    }


TIME_STEP = 0.2
VISCOSITY = 0.5
DRIVE = 0.05
FORCING = 2.0
TWO_PI = 6.283185307179586


def x_ends(field, periodic, inlet):
    if periodic:
        return field[..., -1:, :, :], field[..., :1, :, :]
    if inlet is None:
        empty = jnp.zeros_like(field[..., :1, :, :])
        return empty, empty
    return inlet[:, None], field[:, -1:]


def neighbours(field, ext, low, high):
    along = jnp.concatenate([low, field, high], axis=-3)
    return (along[..., :-2, :, :], along[..., 2:, :, :],
            ext[..., :-2, 1:-1], ext[..., 2:, 1:-1],
            ext[..., 1:-1, :-2], ext[..., 1:-1, 2:])


def rim(field):
    ndims = field.ndim
    wrapped = jnp.pad(field, [(0, 0)] * (ndims - 2) + [(1, 1), (0, 0)], mode="wrap")
    return jnp.pad(wrapped, [(0, 0)] * (ndims - 1) + [(1, 1)])


def sweep(ext, source, periodic):
    center = ext[..., 1:-1, 1:-1]
    low, high = x_ends(center, periodic, None)
    xm, xp, ym, yp, zm, zp = neighbours(center, ext, low, high)
    return (((xm + xp) + (ym + yp)) + (zm + zp) - source) / 6.0


def advance(velocity, force, periodic, inlet):
    low, high = x_ends(velocity, periodic, inlet)
    xm, xp, ym, yp, zm, zp = neighbours(velocity, rim(velocity), low, high)
    carried = velocity[0:1] * (xp - xm) * 0.5 + velocity[1:2] * (yp - ym) * 0.5 + velocity[2:3] * (zp - zm) * 0.5
    spread = ((xm + xp) + (ym + yp)) + (zm + zp) - 6.0 * velocity
    provisional = velocity + TIME_STEP * (VISCOSITY * spread - carried + force)
    low, high = x_ends(provisional, periodic, inlet)
    along = jnp.concatenate([low[0:1], provisional[0:1], high[0:1]], axis=1)
    ext = rim(provisional[1:3])
    diverge = 0.5 * ((along[0, 2:] - along[0, :-2]) + (ext[0, :, 2:, 1:-1] - ext[0, :, :-2, 1:-1])
                     + (ext[1, :, 1:-1, 2:] - ext[1, :, 1:-1, :-2]))
    source = diverge / TIME_STEP
    pressure = jnp.zeros_like(source)
    for count in range(SWEEPS):
        pressure = sweep(rim(pressure), source, periodic)
    low, high = x_ends(pressure, periodic, None)
    xm, xp, ym, yp, zm, zp = neighbours(pressure, rim(pressure), low, high)
    push = jnp.stack([xp - xm, yp - ym, zp - zm])
    return provisional - TIME_STEP * 0.5 * push


def reference(pre_velocity, deck_velocity, deck_force, inlet_shift, tap_offset, tap_weight, phase_index):
    drive = jnp.array([DRIVE, 0.0, 0.0], jnp.float32).reshape(3, 1, 1, 1)
    halves = jnp.arange(NYM, dtype=jnp.int32) // 2
    precursor, deck = pre_velocity, deck_velocity
    for step in range(STEPS):
        precursor = advance(precursor, drive, True, None)
        plane = precursor[:, -1]
        targets = ((halves[:, None] + inlet_shift[step] + tap_offset) % NYP).astype(jnp.int32)
        inlet = tap_weight[None, :, 0:1] * plane[:, targets[:, 0], :]
        for tap in range(1, TAPS):
            inlet = inlet + tap_weight[None, :, tap:tap + 1] * plane[:, targets[:, tap], :]
        amplitude = jnp.sin(TWO_PI * phase_index[step].astype(jnp.float32) / PERIOD)
        zeros = jnp.zeros_like(deck_force)
        force = jnp.stack([zeros, zeros, FORCING * amplitude * deck_force])
        deck = advance(deck, force, False, inlet)
    return precursor, deck
```

```python
import functools

import jax
import jax.numpy as jnp
from jax import lax
from jax.experimental import pallas as pl
from jax.experimental.pallas import tpu as pltpu
from jax.sharding import PartitionSpec as P

STEPS = 4
SWEEPS = 7
PERIOD = 64
TIME_STEP = 0.2
VISCOSITY = 0.5
DRIVE = 0.05
FORCING = 2.0
TWO_PI = 6.283185307179586

MESH = pl.DeviceIdType.MESH
X = 16
LANES = 128
REACH = SWEEPS + 2
SLOT = 4
BLOCK = 8
NEAR = 8


def pad4(depth):
    return -(-depth // SLOT) * SLOT


class Grid:
    def __init__(self, rows, depth, periodic, refs):
        self.n, self.depth, self.periodic = rows, depth, periodic
        self.base = pad4(depth)
        self.x0 = 0 if periodic else 8
        self.u, self.v, self.pa, self.pb, self.s = refs

    @staticmethod
    def scratch(rows, depth, periodic, comps):
        total = rows + 2 * pad4(depth)
        subs = X if periodic else 32
        field = pltpu.VMEM((2, total, subs, LANES), jnp.float32)
        return [
            pltpu.VMEM((comps, 2, total, subs, LANES), jnp.float32),
            pltpu.VMEM((3, 2, total, subs, LANES), jnp.float32),
            field,
            field,
            pltpu.VMEM((2, total, X, LANES), jnp.float32),
        ]

    def at(self, ref, *index):
        if self.periodic:
            return ref[index]
        return ref[index + (slice(8, 24), slice(None))]

    def xs(self, ref, center, *index):
        if self.periodic:
            return pltpu.roll(center, 1, 0), pltpu.roll(center, X - 1, 0)
        return ref[index + (slice(7, 23), slice(None))], ref[index + (slice(9, 25), slice(None))]

    def put(self, ref, value, *index):
        if self.periodic:
            ref[index] = value
        else:
            ref[index + (slice(8, 24), slice(None))] = value

    def put_high(self, ref, value, *index):
        if not self.periodic:
            ref[index + (slice(24, 25), slice(None))] = value[X - 1 : X]


def loop_rows(low, high, body, width=2):
    count = (high - low) // width

    def run(k, carry):
        body(low + k * width)
        return carry

    lax.fori_loop(0, count, run, 0)
    if count * width < high - low:
        body(low + count * width, high - low - count * width)


def z_pair(parity, even, odd):
    if parity == 0:
        return pltpu.roll(odd, 1, 1), odd
    return even, pltpu.roll(even, LANES - 1, 1)


def advance(g, depth, masks, force):
    lo, hi = g.base - depth, g.base + g.n + depth

    def provisional(i, width=2):
        for row in range(width):
            r = i + row
            mid = [[g.at(g.u, c, q, r) for q in range(2)] for c in range(3)]
            for q in range(2):
                less = [1.0 - mid[c][q] for c in range(3)]
                more = [1.0 + mid[c][q] for c in range(3)]
                for c in range(3):
                    u = mid[c][q]
                    xm, xp = g.xs(g.u, u, c, q, r)
                    ym, yp = g.at(g.u, c, q, r - 1), g.at(g.u, c, q, r + 1)
                    zm, zp = z_pair(q, mid[c][0], mid[c][1])
                    around = (less[0] * xp + more[0] * xm) + (less[1] * yp + more[1] * ym)
                    around = around + (less[2] * zp + more[2] * zm)
                    value = (1.0 - 6.0 * TIME_STEP * VISCOSITY) * u + (TIME_STEP * VISCOSITY) * around
                    value = force(value, c, q, r) * masks[q]
                    g.put(g.v, value, c, q, r)
                    if c == 0:
                        g.put_high(g.v, value, c, q, r)

    loop_rows(lo + 1, hi - 1, provisional)

    def source(i, width=2):
        for row in range(width):
            r = i + row
            vz = [g.at(g.v, 2, q, r) for q in range(2)]
            for q in range(2):
                xm, xp = g.xs(g.v, g.at(g.v, 0, q, r) if g.periodic else None, 0, q, r)
                zm, zp = z_pair(q, vz[0], vz[1])
                total = (xp - xm) + (g.at(g.v, 1, q, r + 1) - g.at(g.v, 1, q, r - 1)) + (zp - zm)
                value = total * (masks[q] * (0.5 / TIME_STEP / 6.0))
                g.s[q, r] = value
                g.put(g.pa, -value, q, r)

    loop_rows(lo + 2, hi - 2, source)

    sixth = [m * (1.0 / 6.0) for m in masks]
    src, dst = g.pa, g.pb
    for k in range(1, SWEEPS):

        def sweep(i, width=2, src=src, dst=dst):
            mid = [[g.at(src, q, i + row) for q in range(2)] for row in range(-1, width + 1)]
            for row in range(width):
                for q in range(2):
                    center = mid[row + 1][q]
                    xm, xp = g.xs(src, center, q, i + row)
                    zm, zp = z_pair(q, mid[row + 1][0], mid[row + 1][1])
                    total = ((xm + xp) + (mid[row][q] + mid[row + 2][q])) + (zm + zp)
                    g.put(dst, total * sixth[q] - g.s[q, i + row], q, i + row)

        loop_rows(lo + 2 + k, hi - 2 - k, sweep)
        src, dst = dst, src

    def correct(i, width=2):
        mid = [[g.at(src, q, i + row) for q in range(2)] for row in range(-1, width + 1)]
        for row in range(width):
            r = i + row
            for q in range(2):
                xm, xp = g.xs(src, mid[row + 1][q], q, r)
                zm, zp = z_pair(q, mid[row + 1][0], mid[row + 1][1])
                slopes = (xp - xm, mid[row + 2][q] - mid[row][q], zp - zm)
                scale = masks[q] * (TIME_STEP * 0.5)
                for c in range(3):
                    value = g.at(g.v, c, q, r) - scale * slopes[c]
                    g.put(g.u, value, c, q, r)
                    g.put_high(g.u, value, c, q, r)

    loop_rows(lo + REACH, hi - REACH, correct)


def select4(slot, pieces):
    out = pieces[3]
    for s in (2, 1, 0):
        out = jnp.where(slot == s, pieces[s], out)
    return out


class Halo:
    def __init__(self, g, comps, depth, refs):
        self.g, self.comps, self.depth = g, comps, depth
        self.rm, self.left, self.right, self.to_left, self.to_right = refs
        self.copies = []

    @staticmethod
    def scratch(rows, depth, comps):
        total = rows + 2 * pad4(depth)
        edge = pltpu.VMEM((comps, total // SLOT, X, LANES), jnp.float32)
        own = pltpu.VMEM((comps, rows // SLOT, X, LANES), jnp.float32)
        return [pltpu.VMEM((comps, total, X, LANES), jnp.float32), edge, edge, own, own]

    @staticmethod
    def plan(rows, depth):
        out = []
        for dm in range(-4, 5):
            first, end = max(0, rows * dm - depth), min(rows, rows * dm + rows + depth)
            if first < end:
                out.append((dm, first, end))
        return out

    def pack(self, lane):
        g, base = self.g, pad4(self.depth)
        edges = (lane < 48) | ((lane >= 64) & (lane < 96))
        slot = lane // 32
        spare = base - self.depth
        for c in range(self.comps):
            for k in range(spare):
                self.rm[c, k] = jnp.zeros((X, LANES), jnp.float32)
                self.rm[c, 2 * base + g.n - 1 - k] = jnp.zeros((X, LANES), jnp.float32)

        def block(b, carry):
            for c in range(self.comps):
                lefts, rights = [], []
                for s in range(SLOT):
                    r = b * SLOT + s
                    even, odd = g.at(g.u, c, 0, g.base + r), g.at(g.u, c, 1, g.base + r)
                    self.rm[c, base + r] = jnp.where(lane < 64, pltpu.roll(even, 96, 1), pltpu.roll(odd, 32, 1))
                    both = jnp.where(edges, even, pltpu.roll(odd, 16, 1))
                    lefts.append(pltpu.roll(both, (32 * s - 32) % LANES, 1))
                    rights.append(pltpu.roll(both, (32 * s - 80) % LANES, 1))
                self.to_left[c, b] = select4(slot, lefts)
                self.to_right[c, b] = select4(slot, rights)
            return carry

        lax.fori_loop(0, g.n // SLOT, block, 0)

    def send(self, net):
        g, base = self.g, pad4(self.depth)
        for dm, first, end in self.plan(g.n, self.depth):
            start = base + first - g.n * dm
            if dm:
                net.send(
                    self.rm.at[:, pl.ds(base + first, end - first)],
                    self.rm.at[:, pl.ds(start, end - first)],
                    0,
                    dm,
                    self.copies,
                )
            low, high = first // SLOT, -(-end // SLOT)
            there = base // SLOT + low - g.n // SLOT * dm
            for dp, mine, theirs in ((-1, self.to_left, self.right), (1, self.to_right, self.left)):
                net.send(
                    mine.at[:, pl.ds(low, high - low)],
                    theirs.at[:, pl.ds(there, high - low)],
                    dp,
                    dm,
                    self.copies,
                )

    def finish(self, lane, masks):
        g, base = self.g, pad4(self.depth)
        for copy in self.copies:
            copy.wait_recv()
        total = g.n + 2 * base
        shift = g.base - base
        inner = (lane >= 32) & (lane < 96)
        low = lane < 32

        def block(b, carry):
            for c in range(self.comps):
                left, right = self.left[c, b], self.right[c, b]
                for s in range(SLOT):
                    r = b * SLOT + s
                    row = self.rm[c, r]
                    for q, turn in ((0, 32), (1, 96)):
                        a = pltpu.roll(left, (16 - 16 * q - 32 * s) % LANES, 1)
                        z = pltpu.roll(right, (96 - 16 * q - 32 * s) % LANES, 1)
                        value = jnp.where(inner, pltpu.roll(row, turn, 1), jnp.where(low, a, z)) * masks[q]
                        g.put(g.u, value, c, q, r + shift)
                        g.put_high(g.u, value, c, q, r + shift)
            return carry

        lax.fori_loop(0, total // SLOT, block, 0)


class Net:
    def __init__(self, sems_out, sems_in):
        self.out, self.into, self.count, self.all = sems_out, sems_in, 0, []
        self.p, self.m = lax.axis_index("pre"), lax.axis_index("main")
        self.np, self.nm = lax.axis_size("pre"), lax.axis_size("main")

    def device(self, dp, dm):
        return (lax.rem(self.p + dp + self.np, self.np), lax.rem(self.m + dm + self.nm, self.nm))

    def send(self, src, dst, dp, dm, copies):
        copy = pltpu.make_async_remote_copy(
            src_ref=src,
            dst_ref=dst,
            send_sem=self.out.at[self.count],
            recv_sem=self.into.at[self.count],
            device_id=self.device(dp, dm),
            device_id_type=MESH,
        )
        self.count += 1
        copy.start()
        copies.append(copy)
        self.all.append(copy)


PRE_ROWS, DECK_ROWS = 8, 16
PRE_DEPTHS = (9, 9, 9, 9)
DECK_DEPTHS = (9, 9, 9, 9)
PRE_MAX, DECK_MAX = max(PRE_DEPTHS), max(DECK_DEPTHS)
DECK_BASE = pad4(DECK_MAX)
REACH_LOW = -((-(DECK_MAX + 1) // 2 - 1) // BLOCK)
REACH_HIGH = ((DECK_ROWS + DECK_MAX - 1) // 2 + 2 + BLOCK - 1) // BLOCK
NEAR_LOW, NEAR_HIGH = -NEAR // 2 - REACH_LOW, NEAR // 2 - 1 + REACH_HIGH


def neighbours_of_all(far):
    out = set()
    for rows, depths in ((PRE_ROWS, PRE_DEPTHS), (DECK_ROWS, DECK_DEPTHS)):
        for depth in depths:
            for dm, _, _ in Halo.plan(rows, depth):
                out |= {(dp, dm) for dp in (-1, 0, 1)}
    out |= {(0, d) for d in range(NEAR_LOW, NEAR_HIGH + 1)}
    out |= {(0, -d) for d in range(NEAR_LOW, NEAR_HIGH + 1)}
    out |= {(0, NEAR * h) for h in range(-(far // 2) + 1, far // 2 + 1)}
    out.discard((0, 0))
    return sorted(out)


def kernel(
    far, exchanges, pre_in, deck_in, force_in, taps_in, shifts, amplitudes, pre_out, deck_out, *scratch
):
    scratch = list(scratch)

    def take(count):
        got = scratch[:count]
        del scratch[:count]
        return got

    sems_out, sems_in = take(2)
    pre = Grid(PRE_ROWS, PRE_MAX, True, take(5))
    deck = Grid(DECK_ROWS, DECK_MAX, False, take(5))
    pre_halos = [Halo(pre, 3, d, take(5)) for d in PRE_DEPTHS]
    deck_halos = []
    for t, d in enumerate(DECK_DEPTHS):
        if t == 0 or d > DECK_DEPTHS[t - 1] - REACH:
            deck_halos.append(Halo(deck, 4 if t == 0 else 3, d, take(5)))
        else:
            deck_halos.append(None)
    (taps,) = take(1)
    planes = [take(3) for _ in range(STEPS)]
    pre_flat, deck_flat, force_flat = take(3)

    taps[...] = jnp.zeros(taps.shape, jnp.float32)
    taps[pl.ds(DECK_BASE, DECK_ROWS)] = taps_in[...]
    net = Net(sems_out, sems_in)
    barrier = pltpu.get_barrier_semaphore()
    peers = neighbours_of_all(far)
    for dp, dm in peers:
        pl.semaphore_signal(barrier, inc=1, device_id=net.device(dp, dm), device_id_type=MESH)

    lane = lax.broadcasted_iota(jnp.int32, (X, LANES), 1)
    masks = []
    for q in range(2):
        place = net.p * LANES + (lane - 32) * 2 + q
        masks.append(jnp.where((place >= 0) & (place < net.np * LANES), 1.0, 0.0))

    z_of = lax.broadcasted_iota(jnp.int32, (LANES, LANES), 0)
    l_of = lax.broadcasted_iota(jnp.int32, (LANES, LANES), 1)
    sort = jnp.where(z_of == jnp.where(l_of < 64, 2 * l_of, 2 * l_of - 127), 1.0, 0.0)
    unsort = jnp.where(l_of == jnp.where(z_of < 64, 2 * z_of, 2 * z_of - 127), 1.0, 0.0)

    def load(g, source, flat, comps, first):
        for c in range(comps):
            flat[c] = jnp.dot(
                source[pl.ds(c * X * g.n, X * g.n)],
                sort,
                precision=lax.Precision.HIGHEST,
                preferred_element_type=jnp.float32,
            )

            def row(r, carry):
                value = flat[c, pl.ds(r, X, stride=g.n)]
                g.put(g.u, pltpu.roll(value, 32, 1), first + c, 0, g.base + r)
                g.put(g.u, pltpu.roll(value, 96, 1), first + c, 1, g.base + r)
                return carry

            lax.fori_loop(0, g.n, row, 0)

    load(pre, pre_in, pre_flat, 3, 0)
    pre_halos[0].pack(lane)
    pl.semaphore_wait(barrier, len(peers))
    pre_halos[0].send(net)
    load(deck, deck_in, deck_flat, 3, 0)
    load(deck, force_in, force_flat, 1, 3)
    for ref in (deck.pa, deck.pb):
        ref[...] = jnp.zeros(ref.shape, jnp.float32)
    deck_halos[0].pack(lane)
    deck_halos[0].send(net)
    tap_copies = []
    for dm, first, end in Halo.plan(DECK_ROWS, DECK_MAX):
        if dm:
            net.send(
                taps.at[pl.ds(DECK_BASE + first, end - first)],
                taps.at[pl.ds(DECK_BASE + first - DECK_ROWS * dm, end - first)],
                0,
                dm,
                tap_copies,
            )

    def pre_force(value, c, q, r):
        return value + TIME_STEP * DRIVE if c == 0 else value

    def precursor_step(t):
        pre_halos[t].finish(lane, masks)
        advance(pre, PRE_DEPTHS[t], masks, pre_force)
        if t + 1 < STEPS:
            pre_halos[t + 1].pack(lane)
            pre_halos[t + 1].send(net)
        block, hop, near = planes[t]

        def row(r, carry):
            for c in range(3):
                for q in range(2):
                    k = 2 * c + q
                    block[r, k : k + 1] = pre.u[c, q, pre.base + r, X - 1 : X]
            block[r, 6:8] = jnp.zeros((2, LANES), jnp.float32)
            return carry

        lax.fori_loop(0, BLOCK, row, 0)
        hop[0] = block[...]
        copies = []
        for h in range(1, far):
            back = -NEAR * h if h <= far // 2 else NEAR * (far - h)
            net.send(block, hop.at[h], 0, back, copies)
        return copies

    def shift_of(t):
        total = BLOCK * net.nm
        moved = lax.rem(shifts[t] + BLOCK * NEAR // 2, total)
        turn = moved // (BLOCK * NEAR)
        return turn, moved - turn * (BLOCK * NEAR) - BLOCK * NEAR // 2

    def near_hop(t, copies):
        _, hop, near = planes[t]
        for copy in copies:
            copy.wait_recv()
        turn, _ = shift_of(t)
        near[pl.ds(-NEAR_LOW * BLOCK, BLOCK)] = hop[turn]
        out = []
        for d in range(NEAR_LOW, NEAR_HIGH + 1):
            if d:
                net.send(
                    near.at[pl.ds(-NEAR_LOW * BLOCK, BLOCK)],
                    near.at[pl.ds((d - NEAR_LOW) * BLOCK, BLOCK)],
                    0,
                    -d,
                    out,
                )
        return out

    def inlet(t, copies):
        _, _, near = planes[t]
        for copy in copies:
            copy.wait_recv()
        _, rest = shift_of(t)
        depth = DECK_DEPTHS[t]
        start = -(-depth // 2) * 2
        origin = rest - NEAR_LOW * BLOCK - start // 2 - 1

        def pair(k, carry):
            rows = [near[origin + k + d] for d in range(4)]
            for odd in range(2):
                r = DECK_BASE - start + 2 * k + odd
                weights = taps[r]
                value = weights[0:1] * rows[0]
                for d in range(1, 4):
                    value = value + weights[d : d + 1] * rows[d]
                for c in range(3):
                    for q in range(2):
                        deck.u[c, q, r, 7:8] = value[2 * c + q : 2 * c + q + 1]
                for q in range(2):
                    deck.v[0, q, r, 7:8] = value[q : q + 1]
            return carry

        lax.fori_loop(0, (DECK_ROWS + 2 * start) // 2, pair, 0)

    def deck_step(t):
        gain = amplitudes[t]

        def deck_force(value, c, q, r):
            return value + gain * deck.at(deck.u, 3, q, r) if c == 2 else value

        if deck_halos[t] is not None:
            deck_halos[t].finish(lane, masks)
        advance(deck, DECK_DEPTHS[t], masks, deck_force)
        if t + 1 < STEPS and deck_halos[t + 1] is not None:
            deck_halos[t + 1].pack(lane)
            deck_halos[t + 1].send(net)

    far_copies = {0: precursor_step(0)}
    near_copies = {0: near_hop(0, far_copies[0])}
    for copy in tap_copies:
        copy.wait_recv()
    for t in range(STEPS):
        if t + 1 < STEPS:
            far_copies[t + 1] = precursor_step(t + 1)
        inlet(t, near_copies[t])
        deck_step(t)
        if t + 1 < STEPS:
            near_copies[t + 1] = near_hop(t + 1, far_copies[t + 1])

    def store(g, flat, target):
        for c in range(3):

            def row(r, carry):
                even, odd = g.at(g.u, c, 0, g.base + r), g.at(g.u, c, 1, g.base + r)
                both = jnp.where(lane < 64, pltpu.roll(even, 96, 1), pltpu.roll(odd, 32, 1))
                flat[c, pl.ds(r, X, stride=g.n)] = both
                return carry

            lax.fori_loop(0, g.n, row, 0)
            target[pl.ds(c * X * g.n, X * g.n)] = jnp.dot(
                flat[c], unsort, precision=lax.Precision.HIGHEST, preferred_element_type=jnp.float32
            )

    store(pre, pre_flat, pre_out)
    store(deck, deck_flat, deck_out)
    for copy in net.all:
        copy.wait_send()


def message_count(far):
    count = 0
    for rows, depths in ((PRE_ROWS, PRE_DEPTHS), (DECK_ROWS, DECK_DEPTHS)):
        for depth in depths:
            count += 3 * len(Halo.plan(rows, depth))
    count += len(Halo.plan(DECK_ROWS, DECK_MAX))
    return count + STEPS * (far - 1 + NEAR_HIGH - NEAR_LOW)


def shards(pre_velocity, deck_velocity, deck_force, inlet_shift, tap_offset, tap_weight, phase_index):
    far = lax.axis_size("main") // NEAR
    steps_of = jnp.arange(-1, 3, dtype=jnp.int32)
    hits = tap_offset[:, :, None] == steps_of
    taps = jnp.sum(jnp.where(hits, tap_weight[:, :, None], 0.0), axis=1)
    taps = jnp.concatenate([taps, jnp.zeros_like(taps)], axis=1)
    taps = jnp.broadcast_to(taps[:, :, None], taps.shape + (LANES,))
    amplitude = jnp.sin(TWO_PI * phase_index.astype(jnp.float32) / PERIOD)
    gains = TIME_STEP * FORCING * amplitude

    vmem = pl.BlockSpec(memory_space=pltpu.VMEM)
    smem = pl.BlockSpec(memory_space=pltpu.SMEM)
    messages = message_count(far)
    scratch = [pltpu.SemaphoreType.DMA((messages,)), pltpu.SemaphoreType.DMA((messages,))]
    scratch += Grid.scratch(PRE_ROWS, PRE_MAX, True, 3)
    scratch += Grid.scratch(DECK_ROWS, DECK_MAX, False, 4)
    for depth in PRE_DEPTHS:
        scratch += Halo.scratch(PRE_ROWS, depth, 3)
    for t, depth in enumerate(DECK_DEPTHS):
        if t == 0 or depth > DECK_DEPTHS[t - 1] - REACH:
            scratch += Halo.scratch(DECK_ROWS, depth, 4 if t == 0 else 3)
    scratch.append(pltpu.VMEM((DECK_ROWS + 2 * DECK_BASE, 8, LANES), jnp.float32))
    for _ in range(STEPS):
        scratch.append(pltpu.VMEM((BLOCK, 8, LANES), jnp.float32))
        scratch.append(pltpu.VMEM((far, BLOCK, 8, LANES), jnp.float32))
        scratch.append(pltpu.VMEM(((NEAR_HIGH - NEAR_LOW + 1) * BLOCK, 8, LANES), jnp.float32))
    scratch.append(pltpu.VMEM((3, X * PRE_ROWS, LANES), jnp.float32))
    scratch.append(pltpu.VMEM((3, X * DECK_ROWS, LANES), jnp.float32))
    scratch.append(pltpu.VMEM((1, X * DECK_ROWS, LANES), jnp.float32))

    pre_rows, deck_rows = 3 * X * PRE_ROWS, 3 * X * DECK_ROWS
    pre, deck = pl.pallas_call(
        functools.partial(kernel, far, None),
        out_shape=(
            jax.ShapeDtypeStruct((pre_rows, LANES), jnp.float32),
            jax.ShapeDtypeStruct((deck_rows, LANES), jnp.float32),
        ),
        in_specs=[vmem, vmem, vmem, vmem, smem, smem],
        out_specs=(vmem, vmem),
        scratch_shapes=scratch,
        compiler_params=pltpu.CompilerParams(
            collective_id=0, has_side_effects=True, vmem_limit_bytes=56 * 1024 * 1024
        ),
    )(
        pre_velocity.reshape(pre_rows, LANES),
        deck_velocity.reshape(deck_rows, LANES),
        deck_force.reshape(X * DECK_ROWS, LANES),
        taps,
        inlet_shift,
        gains,
    )
    return pre.reshape(pre_velocity.shape), deck.reshape(deck_velocity.shape)


def solution(mesh):
    placed = (
        P(None, None, "main", "pre"),
        P(None, None, "main", "pre"),
        P(None, "main", "pre"),
        P(),
        P("main", None),
        P("main", None),
        P(),
    )
    return jax.shard_map(
        shards,
        mesh=mesh,
        in_specs=placed,
        out_specs=(P(None, None, "main", "pre"), P(None, None, "main", "pre")),
        check_vma=False,
    )
```

```python
import functools

import jax
import jax.numpy as jnp
from jax import lax
from jax.experimental import pallas as pl
from jax.experimental.pallas import tpu as pltpu
from jax.sharding import PartitionSpec as P

STEPS = 4
SWEEPS = 7
PERIOD = 64
TIME_STEP = 0.2
VISCOSITY = 0.5
DRIVE = 0.05
FORCING = 2.0
TWO_PI = 6.283185307179586

MESH = pl.DeviceIdType.MESH
X = 16
LANES = 128
REACH = SWEEPS + 2
SLOT = 8
WIDTH = 8
BLOCK = 8
NEAR = 8


def padded(depth):
    return -(-depth // SLOT) * SLOT


class Grid:
    def __init__(self, rows, depth, periodic, refs):
        self.n, self.depth, self.periodic = rows, depth, periodic
        self.base = padded(depth)
        self.u, self.v, self.pa, self.pb, self.s = refs

    @staticmethod
    def scratch(rows, depth, periodic, comps):
        total = rows + 2 * padded(depth)
        subs = X if periodic else 32
        field = pltpu.VMEM((2, total, subs, LANES), jnp.float32)
        return [
            pltpu.VMEM((comps, 2, total, subs, LANES), jnp.float32),
            pltpu.VMEM((3, 2, total, subs, LANES), jnp.float32),
            field,
            field,
            pltpu.VMEM((2, total, X, LANES), jnp.float32),
        ]

    def at(self, ref, *index):
        if self.periodic:
            return ref[index]
        return ref[index + (slice(8, 24), slice(None))]

    def xs(self, ref, center, *index):
        if self.periodic:
            return pltpu.roll(center, 1, 0), pltpu.roll(center, X - 1, 0)
        return ref[index + (slice(7, 23), slice(None))], ref[index + (slice(9, 25), slice(None))]

    def put(self, ref, value, *index):
        if self.periodic:
            ref[index] = value
        else:
            ref[index + (slice(8, 24), slice(None))] = value

    def put_high(self, ref, value, *index):
        if not self.periodic:
            ref[index + (slice(24, 25), slice(None))] = value[X - 1 : X]


def loop_rows(low, high, body, width=WIDTH):
    count = (high - low) // width

    def run(k, carry):
        body(low + k * width, width)
        return carry

    if count > 1:
        lax.fori_loop(0, count, run, 0)
    elif count:
        body(low, width)
    if count * width < high - low:
        body(low + count * width, high - low - count * width)


def z_pair(parity, even, odd):
    if parity == 0:
        return pltpu.roll(odd, 1, 1), odd
    return even, pltpu.roll(even, LANES - 1, 1)


def solve(g, depth, spare, masks, force):
    lo, hi = g.base - depth, g.base + g.n + depth

    def provisional(i, width):
        for row in range(width):
            r = i + row
            mid = [[g.at(g.u, c, q, r) for q in range(2)] for c in range(3)]
            for q in range(2):
                less = [1.0 - mid[c][q] for c in range(3)]
                more = [1.0 + mid[c][q] for c in range(3)]
                for c in range(3):
                    u = mid[c][q]
                    xm, xp = g.xs(g.u, u, c, q, r)
                    ym, yp = g.at(g.u, c, q, r - 1), g.at(g.u, c, q, r + 1)
                    zm, zp = z_pair(q, mid[c][0], mid[c][1])
                    around = (less[0] * xp + more[0] * xm) + (less[1] * yp + more[1] * ym)
                    around = around + (less[2] * zp + more[2] * zm)
                    value = (1.0 - 6.0 * TIME_STEP * VISCOSITY) * u + (TIME_STEP * VISCOSITY) * around
                    value = force(value, c, q, r) * masks[q]
                    g.put(g.v, value, c, q, r)
                    if c == 0:
                        g.put_high(g.v, value, c, q, r)

    loop_rows(lo + 1, hi - 1, provisional, 4)

    reach = SWEEPS - 1 + spare
    lo, hi = g.base - reach, g.base + g.n + reach

    def source(i, width):
        for row in range(width):
            r = i + row
            vz = [g.at(g.v, 2, q, r) for q in range(2)]
            for q in range(2):
                xm, xp = g.xs(g.v, g.at(g.v, 0, q, r) if g.periodic else None, 0, q, r)
                zm, zp = z_pair(q, vz[0], vz[1])
                total = (xp - xm) + (g.at(g.v, 1, q, r + 1) - g.at(g.v, 1, q, r - 1)) + (zp - zm)
                value = total * (masks[q] * (0.5 / TIME_STEP / 6.0))
                g.s[q, r] = value
                g.put(g.pa, -value, q, r)

    loop_rows(lo, hi, source)

    sixth = [m * (1.0 / 6.0) for m in masks]
    src, dst = g.pa, g.pb
    for k in range(1, SWEEPS):

        def sweep(i, width, src=src, dst=dst):
            mid = [[g.at(src, q, i + row) for q in range(2)] for row in range(-1, width + 1)]
            for row in range(width):
                for q in range(2):
                    center = mid[row + 1][q]
                    xm, xp = g.xs(src, center, q, i + row)
                    zm, zp = z_pair(q, mid[row + 1][0], mid[row + 1][1])
                    total = ((xm + xp) + (mid[row][q] + mid[row + 2][q])) + (zm + zp)
                    g.put(dst, total * sixth[q] - g.s[q, i + row], q, i + row)

        loop_rows(lo + k, hi - k, sweep)
        src, dst = dst, src


def correct(g, depth, masks):
    scales = [m * (TIME_STEP * 0.5) for m in masks]

    def rows(i, width):
        mid = [[g.at(g.pa, q, i + row) for q in range(2)] for row in range(-1, width + 1)]
        for row in range(width):
            r = i + row
            for q in range(2):
                xm, xp = g.xs(g.pa, mid[row + 1][q], q, r)
                zm, zp = z_pair(q, mid[row + 1][0], mid[row + 1][1])
                slopes = (xp - xm, mid[row + 2][q] - mid[row][q], zp - zm)
                for c in range(3):
                    value = g.at(g.v, c, q, r) - scales[q] * slopes[c]
                    g.put(g.u, value, c, q, r)
                    g.put_high(g.u, value, c, q, r)

    loop_rows(g.base - depth, g.base + g.n + depth, rows, 4)


class Halo:
    def __init__(self, g, comps, depth, refs):
        self.g, self.comps, self.depth = g, comps, depth
        self.rm, self.left, self.right, self.to_left, self.to_right = refs
        self.base = padded(depth)
        self.copies = []

    @staticmethod
    def scratch(rows, depth, comps):
        total = rows + 2 * padded(depth)
        edge = pltpu.VMEM((comps, total // SLOT, X, LANES), jnp.float32)
        own = pltpu.VMEM((comps, rows // SLOT, X, LANES), jnp.float32)
        return [pltpu.VMEM((comps, total, X, LANES), jnp.float32), edge, edge, own, own]

    @staticmethod
    def plan(rows, depth):
        out = []
        for dm in (0, 1, -1, 2, -2, 3, -3):
            first, end = max(0, rows * dm - depth), min(rows, rows * dm + rows + depth)
            if first < end:
                out.append((dm, first, end))
        return out

    def pack(self, lane, c, fetch):
        edges = ((lane >= 32) & (lane < 40)) | ((lane >= 88) & (lane < 96))
        slot_right = lane // 16
        slot_left = lax.rem(lane + 56, LANES) // 16
        for b in range(self.g.n // SLOT):
            lefts = rights = None
            for s in range(SLOT):
                r = b * SLOT + s
                even, odd, merged = fetch(r)
                self.rm[c, self.base + r] = merged
                both = jnp.where(edges, even, pltpu.roll(odd, 8, 1))
                a = pltpu.roll(both, (16 * s + 40) % LANES, 1)
                z = pltpu.roll(both, (16 * s - 88) % LANES, 1)
                lefts = a if s == 0 else jnp.where(slot_left == s, a, lefts)
                rights = z if s == 0 else jnp.where(slot_right == s, z, rights)
            self.to_left[c, b] = lefts
            self.to_right[c, b] = rights

    def send(self, net):
        n, base = self.g.n, self.base
        for dm, first, end in self.plan(n, self.depth):
            start = base + first - n * dm
            if dm:
                net.send(
                    self.rm.at[:, pl.ds(base + first, end - first)],
                    self.rm.at[:, pl.ds(start, end - first)],
                    0,
                    dm,
                    self.copies,
                )
            low, high = first // SLOT, -(-end // SLOT)
            there = base // SLOT + low - n // SLOT * dm
            for dp, mine, theirs in ((-1, self.to_left, self.right), (1, self.to_right, self.left)):
                net.send(
                    mine.at[:, pl.ds(low, high - low)],
                    theirs.at[:, pl.ds(there, high - low)],
                    dp,
                    dm,
                    self.copies,
                )

    def finish(self, lane, c, own, put):
        inner = (lane >= 32) & (lane < 96)
        for r in range(-self.depth, self.g.n + self.depth):
            block, s = (r + self.base) // SLOT, (r + self.base) % SLOT
            mine = (lane >= 16 * s) & (lane < 16 * s + 16)
            outer = jnp.where(mine, self.left[c, block], self.right[c, block])
            kept = own is not None and 0 <= r < self.g.n
            row = None if kept else self.rm[c, r + self.base]
            for q in range(2):
                value = own(q, r) if kept else pltpu.roll(row, 96 if q else 32, 1)
                margin = pltpu.roll(outer, (24 - 8 * q - 16 * s) % LANES, 1)
                put(q, r, jnp.where(inner, value, margin))


class Net:
    def __init__(self, sems_out, sems_in):
        self.out, self.into, self.count, self.all = sems_out, sems_in, 0, []
        self.p, self.m = lax.axis_index("pre"), lax.axis_index("main")
        self.np, self.nm = lax.axis_size("pre"), lax.axis_size("main")

    def device(self, dp, dm):
        return (lax.rem(self.p + dp + self.np, self.np), lax.rem(self.m + dm + self.nm, self.nm))

    def send(self, src, dst, dp, dm, copies):
        copy = pltpu.make_async_remote_copy(
            src_ref=src,
            dst_ref=dst,
            send_sem=self.out.at[self.count],
            recv_sem=self.into.at[self.count],
            device_id=self.device(dp, dm),
            device_id_type=MESH,
        )
        self.count += 1
        copy.start()
        copies.append(copy)
        self.all.append(copy)


PRE_ROWS, DECK_ROWS = 8, 16
DEPTHS = (12, 11, 10, 9)
DEPTH = DEPTHS[0]
ROWS_IN = DECK_ROWS + 2 * 16
WINDOW = 24
FIRST = -7
NEAR_LOW = -(NEAR // 2) + (FIRST // BLOCK)
NEAR_HIGH = NEAR // 2 - 1 + (FIRST + BLOCK - 1 + WINDOW - 1) // BLOCK


def neighbours_of_all(far):
    out = set()
    for rows in (PRE_ROWS, DECK_ROWS):
        for dm, _, _ in Halo.plan(rows, DEPTH):
            out |= {(dp, dm) for dp in (-1, 0, 1)}
    out |= {(0, d) for d in range(NEAR_LOW, NEAR_HIGH + 1)}
    out |= {(0, -d) for d in range(NEAR_LOW, NEAR_HIGH + 1)}
    out |= {(0, NEAR * h) for h in range(-(far // 2) + 1, far // 2 + 1)}
    out.discard((0, 0))
    return sorted(out)


def kernel(far, pre_in, deck_in, force_in, taps_in, shifts, amplitudes, pre_out, deck_out, *scratch):
    scratch = list(scratch)

    def take(count):
        got = scratch[:count]
        del scratch[:count]
        return got

    sems_out, sems_in = take(2)
    pre = Grid(PRE_ROWS, DEPTH, True, take(5))
    deck = Grid(DECK_ROWS, DEPTH, False, take(5))
    pre_halos = [Halo(pre, 1 if t else 3, d, take(5)) for t, d in enumerate((DEPTH,) + DEPTHS[:-1])]
    deck_halos = [Halo(deck, 1 if t else 4, d, take(5)) for t, d in enumerate((DEPTH,) + DEPTHS[:-1])]
    taps, mix = take(2)
    planes = [take(7) for _ in range(STEPS)]
    pre_flat, deck_flat, force_flat = take(3)

    net = Net(sems_out, sems_in)
    barrier = pltpu.get_barrier_semaphore()
    peers = neighbours_of_all(far)
    for dp, dm in peers:
        pl.semaphore_signal(barrier, inc=1, device_id=net.device(dp, dm), device_id_type=MESH)

    lane = lax.broadcasted_iota(jnp.int32, (X, LANES), 1)
    masks = []
    for q in range(2):
        place = net.p * LANES + (lane - 32) * 2 + q
        masks.append(jnp.where((place >= 0) & (place < net.np * LANES), 1.0, 0.0))

    z_of = lax.broadcasted_iota(jnp.int32, (LANES, LANES), 0)
    l_of = lax.broadcasted_iota(jnp.int32, (LANES, LANES), 1)
    sort = jnp.where(z_of == jnp.where(l_of < 64, 2 * l_of, 2 * l_of - 127), 1.0, 0.0)
    unsort = jnp.where(l_of == jnp.where(z_of < 64, 2 * z_of, 2 * z_of - 127), 1.0, 0.0)

    def dot(a, b):
        return jnp.dot(a, b, precision=lax.Precision.HIGHEST, preferred_element_type=jnp.float32)

    def load(halo, source, flat, comps, first):
        n = halo.g.n
        for c in range(comps):
            flat[c] = dot(source[pl.ds(c * X * n, X * n)], sort)

            def fetch(r):
                value = flat[c, pl.ds(r, X, stride=n)]
                return pltpu.roll(value, 32, 1), pltpu.roll(value, 96, 1), value

            halo.pack(lane, first + c, fetch)

    def unload(halo, comps):
        g = halo.g

        def one(c, carry):
            def put(q, r, value):
                value = value * masks[q]
                g.put(g.u, value, c, q, g.base + r)
                g.put_high(g.u, value, c, q, g.base + r)

            halo.finish(lane, c, None, put)
            return carry

        lax.fori_loop(0, comps, one, 0)

    def merge(even, odd, at=lane):
        return jnp.where(at < 64, pltpu.roll(even, 96, 1), pltpu.roll(odd, 32, 1))

    def give_pressure(halo):
        g = halo.g

        def fetch(r):
            even, odd = g.at(g.pa, 0, g.base + r), g.at(g.pa, 1, g.base + r)
            return even, odd, merge(even, odd)

        halo.pack(lane, 0, fetch)
        halo.send(net)

    def take_pressure(halo):
        g = halo.g
        for copy in halo.copies:
            copy.wait_recv()

        def put(q, r, value):
            g.put(g.pa, value * masks[q], q, g.base + r)

        halo.finish(lane, 0, lambda q, r: g.at(g.pa, q, g.base + r), put)
        correct(g, halo.depth - 1, masks)

    load(pre_halos[0], pre_in, pre_flat, 3, 0)
    pl.semaphore_wait(barrier, len(peers))
    pre_halos[0].send(net)
    load(deck_halos[0], deck_in, deck_flat, 3, 0)
    load(deck_halos[0], force_in, force_flat, 1, 3)
    deck_halos[0].send(net)
    tap_copies = []
    taps[pl.ds(16, DECK_ROWS)] = taps_in[...]
    for dm in (1, -1):
        net.send(taps.at[pl.ds(16, 16)], taps.at[pl.ds(16 - 16 * dm, 16)], 0, dm, tap_copies)
    for ref in (deck.pa, deck.pb):
        ref[:, :, 0:8] = jnp.zeros(ref.shape[:2] + (8, LANES), jnp.float32)
        ref[:, :, 24:32] = jnp.zeros(ref.shape[:2] + (8, LANES), jnp.float32)

    def pre_force(value, c, q, r):
        return value + TIME_STEP * DRIVE if c == 0 else value

    def precursor_step(t):
        if t == 0:
            for copy in pre_halos[0].copies:
                copy.wait_recv()
            unload(pre_halos[0], 3)
        else:
            take_pressure(pre_halos[t])
        solve(pre, DEPTHS[t], 1, masks, pre_force)
        if t + 1 < STEPS:
            give_pressure(pre_halos[t + 1])
        correct(pre, 0, masks)
        block, hop = planes[t][:2]
        wide = lane[:BLOCK]
        for c in range(3):
            for r in range(BLOCK):
                both = [pre.u[c, q, pre.base + r, X - 1 : X] for q in range(2)]
                block[c, r : r + 1] = merge(both[0], both[1], lane[:1])
        hop[0] = block[...]
        copies = []
        for h in range(1, far):
            back = -NEAR * h if h <= far // 2 else NEAR * (far - h)
            net.send(block, hop.at[h], 0, back, copies)
        return copies

    def shift_of(t):
        total = BLOCK * net.nm
        moved = lax.rem(shifts[t] + BLOCK * NEAR // 2, total)
        turn = moved // (BLOCK * NEAR)
        return turn, moved - turn * (BLOCK * NEAR) - BLOCK * NEAR // 2

    def near_hop(t, copies):
        hop, near = planes[t][1:3]
        for copy in copies:
            copy.wait_recv()
        turn, _ = shift_of(t)
        mine = pl.ds(-NEAR_LOW * BLOCK, BLOCK)
        near[:, mine] = hop[turn]
        out = []
        for d in range(NEAR_LOW, NEAR_HIGH + 1):
            if d:
                net.send(near.at[:, mine], near.at[:, pl.ds((d - NEAR_LOW) * BLOCK, BLOCK)], 0, -d, out)
        return out

    def make_mix():
        for copy in tap_copies:
            copy.wait_recv()
        row = lax.broadcasted_iota(jnp.int32, (ROWS_IN, LANES), 0)
        col = lax.broadcasted_iota(jnp.int32, (ROWS_IN, LANES), 1)
        ahead = col - (row // 2 - 8 - 1 - FIRST)
        weights = taps[...]
        total = jnp.zeros((ROWS_IN, LANES), jnp.float32)
        for d in range(4):
            total = jnp.where(ahead == d, weights[:, d : d + 1], total)
        mix[...] = total

    tall = lax.broadcasted_iota(jnp.int32, (ROWS_IN, LANES), 1)

    def inlet(t, copies):
        _, _, near, held, edges, from_left, from_right = planes[t]
        for copy in copies:
            copy.wait_recv()
        _, rest = shift_of(t)
        origin = rest + (FIRST - NEAR_LOW * BLOCK)
        left = right = jnp.zeros((ROWS_IN, LANES), jnp.float32)
        weights = mix[...][:, :WINDOW]
        for c in range(3):
            value = dot(weights, near[c, pl.ds(origin, WINDOW)])
            held[c] = value
            low = (tall >= 16 * c) & (tall < 16 * c + 8)
            high = (tall >= 16 * c + 8) & (tall < 16 * c + 16)
            left = jnp.where(low, pltpu.roll(value, 16 * c, 1), left)
            left = jnp.where(high, pltpu.roll(value, (16 * c + 8 - 64) % LANES, 1), left)
            right = jnp.where(low, pltpu.roll(value, (16 * c - 56) % LANES, 1), right)
            right = jnp.where(high, pltpu.roll(value, (16 * c + 8 - 120) % LANES, 1), right)
        edges[0] = left
        edges[1] = right
        out = []
        net.send(edges.at[0], from_right, -1, 0, out)
        net.send(edges.at[1], from_left, 1, 0, out)
        return out

    def ghosts(t, copies):
        _, _, _, held, _, from_left, from_right = planes[t]
        for copy in copies:
            copy.wait_recv()
        depth = DEPTHS[t] - 1
        inner = (tall >= 32) & (tall < 96)
        for q in range(2):
            spots = net.p * LANES + (tall - 32) * 2 + q
            inside = jnp.where((spots >= 0) & (spots < net.np * LANES), 1.0, 0.0)
            for c in range(3):
                value = pltpu.roll(held[c], 96 if q else 32, 1)
                low = pltpu.roll(from_left[...], (24 - 16 * c - 8 * q) % LANES, 1)
                high = pltpu.roll(from_right[...], (96 - 16 * c - 8 * q) % LANES, 1)
                value = jnp.where(inner, value, jnp.where(tall < 64, low, high)) * inside
                for r in range(-depth, DECK_ROWS + depth):
                    line = value[r + 16 : r + 17]
                    deck.u[c, q, deck.base + r, 7:8] = line
                    if c == 0:
                        deck.v[c, q, deck.base + r, 7:8] = line

    def deck_step(t, copies):
        gain = amplitudes[t]

        def deck_force(value, c, q, r):
            return value + gain * deck.at(deck.u, 3, q, r) if c == 2 else value

        ghosts(t, copies)
        last = t + 1 == STEPS
        solve(deck, DEPTHS[t], 1 if last else 0, masks, deck_force)
        if last:
            correct(deck, 0, masks)
        else:
            give_pressure(deck_halos[t + 1])

    far_copies = {0: precursor_step(0)}
    for copy in deck_halos[0].copies:
        copy.wait_recv()
    unload(deck_halos[0], 4)
    make_mix()
    near_copies = {0: near_hop(0, far_copies[0])}
    far_copies[1] = precursor_step(1)
    for t in range(STEPS):
        edge_copies = inlet(t, near_copies[t])
        if t:
            take_pressure(deck_halos[t])
        if t + 1 < STEPS:
            near_copies[t + 1] = near_hop(t + 1, far_copies[t + 1])
        deck_step(t, edge_copies)
        if t + 2 < STEPS:
            far_copies[t + 2] = precursor_step(t + 2)

    def store(g, flat, target):
        for c in range(3):
            for r in range(g.n):
                even, odd = g.at(g.u, c, 0, g.base + r), g.at(g.u, c, 1, g.base + r)
                flat[c, pl.ds(r, X, stride=g.n)] = merge(even, odd)
            target[pl.ds(c * X * g.n, X * g.n)] = dot(flat[c], unsort)

    store(pre, pre_flat, pre_out)
    store(deck, deck_flat, deck_out)
    for copy in net.all:
        copy.wait_send()


def message_count(far):
    count = 0
    for rows in (PRE_ROWS, DECK_ROWS):
        for depth in (DEPTH,) + DEPTHS[:-1]:
            count += 3 * len(Halo.plan(rows, depth))
    return count + 2 + STEPS * (far - 1 + NEAR_HIGH - NEAR_LOW + 2)


def shards(pre_velocity, deck_velocity, deck_force, inlet_shift, tap_offset, tap_weight, phase_index):
    far = lax.axis_size("main") // NEAR
    steps_of = jnp.arange(-1, LANES - 1, dtype=jnp.int32)
    hits = tap_offset[:, :, None] == steps_of
    taps = jnp.sum(jnp.where(hits, tap_weight[:, :, None], 0.0), axis=1)
    amplitude = jnp.sin(TWO_PI * phase_index.astype(jnp.float32) / PERIOD)
    gains = TIME_STEP * FORCING * amplitude

    vmem = pl.BlockSpec(memory_space=pltpu.VMEM)
    smem = pl.BlockSpec(memory_space=pltpu.SMEM)
    messages = message_count(far)
    scratch = [pltpu.SemaphoreType.DMA((messages,)), pltpu.SemaphoreType.DMA((messages,))]
    scratch += Grid.scratch(PRE_ROWS, DEPTH, True, 3)
    scratch += Grid.scratch(DECK_ROWS, DEPTH, False, 4)
    for t, depth in enumerate((DEPTH,) + DEPTHS[:-1]):
        scratch += Halo.scratch(PRE_ROWS, depth, 1 if t else 3)
    for t, depth in enumerate((DEPTH,) + DEPTHS[:-1]):
        scratch += Halo.scratch(DECK_ROWS, depth, 1 if t else 4)
    scratch += [pltpu.VMEM((ROWS_IN, LANES), jnp.float32)] * 2
    for _ in range(STEPS):
        scratch.append(pltpu.VMEM((3, BLOCK, LANES), jnp.float32))
        scratch.append(pltpu.VMEM((far, 3, BLOCK, LANES), jnp.float32))
        scratch.append(pltpu.VMEM((3, (NEAR_HIGH - NEAR_LOW + 1) * BLOCK, LANES), jnp.float32))
        scratch.append(pltpu.VMEM((3, ROWS_IN, LANES), jnp.float32))
        scratch.append(pltpu.VMEM((2, ROWS_IN, LANES), jnp.float32))
        scratch += [pltpu.VMEM((ROWS_IN, LANES), jnp.float32)] * 2
    scratch.append(pltpu.VMEM((3, X * PRE_ROWS, LANES), jnp.float32))
    scratch.append(pltpu.VMEM((3, X * DECK_ROWS, LANES), jnp.float32))
    scratch.append(pltpu.VMEM((1, X * DECK_ROWS, LANES), jnp.float32))

    pre_rows, deck_rows = 3 * X * PRE_ROWS, 3 * X * DECK_ROWS
    pre, deck = pl.pallas_call(
        functools.partial(kernel, far),
        out_shape=(
            jax.ShapeDtypeStruct((pre_rows, LANES), jnp.float32),
            jax.ShapeDtypeStruct((deck_rows, LANES), jnp.float32),
        ),
        in_specs=[vmem, vmem, vmem, vmem, smem, smem],
        out_specs=(vmem, vmem),
        scratch_shapes=scratch,
        compiler_params=pltpu.CompilerParams(
            collective_id=0, has_side_effects=True, vmem_limit_bytes=56 * 1024 * 1024
        ),
    )(
        pre_velocity.reshape(pre_rows, LANES),
        deck_velocity.reshape(deck_rows, LANES),
        deck_force.reshape(X * DECK_ROWS, LANES),
        taps,
        inlet_shift,
        gains,
    )
    return pre.reshape(pre_velocity.shape), deck.reshape(deck_velocity.shape)


def solution(mesh):
    placed = (
        P(None, None, "main", "pre"),
        P(None, None, "main", "pre"),
        P(None, "main", "pre"),
        P(),
        P("main", None),
        P("main", None),
        P(),
    )
    return jax.shard_map(
        shards,
        mesh=mesh,
        in_specs=placed,
        out_specs=(P(None, None, "main", "pre"), P(None, None, "main", "pre")),
        check_vma=False,
    )
```

```python
import functools

import jax
import jax.numpy as jnp
from jax import lax
from jax.experimental import pallas as pl
from jax.experimental.pallas import tpu as pltpu
from jax.sharding import PartitionSpec as P

STEPS = 4
SWEEPS = 7
TAPS = 4
PERIOD = 64
TIME_STEP = 0.2
VISCOSITY = 0.5
DRIVE = 0.05
FORCING = 2.0
TWO_PI = 6.283185307179586

MESH = pl.DeviceIdType.MESH
X = 16
LANES = 128
REACH = SWEEPS + 2
SLOT = 8
WIDTH = 16
BLOCK = 8
NEAR = 8


def padded(depth):
    return -(-depth // SLOT) * SLOT


class Grid:
    def __init__(self, rows, depth, periodic, refs):
        self.n, self.depth, self.periodic = rows, depth, periodic
        self.base = padded(depth)
        self.u, self.v, self.pa, self.pb, self.s = refs

    @staticmethod
    def scratch(rows, depth, periodic, comps):
        total = rows + 2 * padded(depth)
        subs = X if periodic else 32
        field = pltpu.VMEM((2, total, subs, LANES), jnp.float32)
        return [
            pltpu.VMEM((comps, 2, total, subs, LANES), jnp.float32),
            pltpu.VMEM((3, 2, total, subs, LANES), jnp.float32),
            field,
            field,
            pltpu.VMEM((2, total, X, LANES), jnp.float32),
        ]

    def at(self, ref, *index):
        if self.periodic:
            return ref[index]
        return ref[index + (slice(8, 24), slice(None))]

    def xs(self, ref, center, *index):
        if self.periodic:
            return pltpu.roll(center, 1, 0), pltpu.roll(center, X - 1, 0)
        return ref[index + (slice(7, 23), slice(None))], ref[index + (slice(9, 25), slice(None))]

    def put(self, ref, value, *index):
        if self.periodic:
            ref[index] = value
        else:
            ref[index + (slice(8, 24), slice(None))] = value

    def put_high(self, ref, value, *index):
        if not self.periodic:
            ref[index + (slice(24, 25), slice(None))] = value[X - 1 : X]


def loop_rows(low, high, body, width=WIDTH):
    count = (high - low) // width

    def run(k, carry):
        body(low + k * width, width)
        return carry

    if count > 1:
        lax.fori_loop(0, count, run, 0)
    elif count:
        body(low, width)
    if count * width < high - low:
        body(low + count * width, high - low - count * width)


def z_pair(parity, even, odd):
    if parity == 0:
        return pltpu.roll(odd, 1, 1), odd
    return even, pltpu.roll(even, LANES - 1, 1)


def solve(g, depth, spare, masks, force, middle=None):
    lo, hi = g.base - depth, g.base + g.n + depth

    def provisional(i, width):
        for row in range(width):
            r = i + row
            mid = [[g.at(g.u, c, q, r) for q in range(2)] for c in range(3)]
            for q in range(2):
                less = [1.0 - mid[c][q] for c in range(3)]
                more = [1.0 + mid[c][q] for c in range(3)]
                for c in range(3):
                    u = mid[c][q]
                    xm, xp = g.xs(g.u, u, c, q, r)
                    ym, yp = g.at(g.u, c, q, r - 1), g.at(g.u, c, q, r + 1)
                    zm, zp = z_pair(q, mid[c][0], mid[c][1])
                    around = (less[0] * xp + more[0] * xm) + (less[1] * yp + more[1] * ym)
                    around = around + (less[2] * zp + more[2] * zm)
                    value = (1.0 - 6.0 * TIME_STEP * VISCOSITY) * u + (TIME_STEP * VISCOSITY) * around
                    value = force(value, c, q, r) * masks[q]
                    g.put(g.v, value, c, q, r)
                    if c == 0:
                        g.put_high(g.v, value, c, q, r)

    loop_rows(lo + 1, hi - 1, provisional, 8)

    reach = SWEEPS - 1 + spare
    lo, hi = g.base - reach, g.base + g.n + reach

    def source(i, width):
        for row in range(width):
            r = i + row
            vz = [g.at(g.v, 2, q, r) for q in range(2)]
            for q in range(2):
                xm, xp = g.xs(g.v, g.at(g.v, 0, q, r) if g.periodic else None, 0, q, r)
                zm, zp = z_pair(q, vz[0], vz[1])
                total = (xp - xm) + (g.at(g.v, 1, q, r + 1) - g.at(g.v, 1, q, r - 1)) + (zp - zm)
                value = total * (masks[q] * (0.5 / TIME_STEP / 6.0))
                g.s[q, r] = value
                g.put(g.pa, -value, q, r)

    loop_rows(lo, hi, source, 8)
    if middle is not None:
        middle()

    sixth = [m * (1.0 / 6.0) for m in masks]
    src, dst = g.pa, g.pb
    for k in range(1, SWEEPS):

        def sweep(i, width, src=src, dst=dst):
            mid = [[g.at(src, q, i + row) for q in range(2)] for row in range(-1, width + 1)]
            for row in range(width):
                for q in range(2):
                    center = mid[row + 1][q]
                    xm, xp = g.xs(src, center, q, i + row)
                    zm, zp = z_pair(q, mid[row + 1][0], mid[row + 1][1])
                    total = ((xm + xp) + (mid[row][q] + mid[row + 2][q])) + (zm + zp)
                    g.put(dst, total * sixth[q] - g.s[q, i + row], q, i + row)

        loop_rows(lo + k, hi - k, sweep)
        src, dst = dst, src


def correct(g, depth, masks):
    scales = [m * (TIME_STEP * 0.5) for m in masks]

    def rows(i, width):
        mid = [[g.at(g.pa, q, i + row) for q in range(2)] for row in range(-1, width + 1)]
        for row in range(width):
            r = i + row
            for q in range(2):
                xm, xp = g.xs(g.pa, mid[row + 1][q], q, r)
                zm, zp = z_pair(q, mid[row + 1][0], mid[row + 1][1])
                slopes = (xp - xm, mid[row + 2][q] - mid[row][q], zp - zm)
                for c in range(3):
                    value = g.at(g.v, c, q, r) - scales[q] * slopes[c]
                    g.put(g.u, value, c, q, r)
                    g.put_high(g.u, value, c, q, r)

    loop_rows(g.base - depth, g.base + g.n + depth, rows, 8)


class Halo:
    def __init__(self, g, comps, depth, refs):
        self.g, self.comps, self.depth = g, comps, depth
        self.rm, self.left, self.right, self.to_left, self.to_right = refs
        self.base = padded(depth)
        self.copies = []

    @staticmethod
    def scratch(rows, depth, comps):
        total = rows + 2 * padded(depth)
        edge = pltpu.VMEM((comps, total // SLOT, X, LANES), jnp.float32)
        own = pltpu.VMEM((comps, rows // SLOT, X, LANES), jnp.float32)
        return [pltpu.VMEM((comps, total, X, LANES), jnp.float32), edge, edge, own, own]

    @staticmethod
    def plan(rows, depth):
        out = []
        for dm in (0, 1, -1, 2, -2, 3, -3):
            first, end = max(0, rows * dm - depth), min(rows, rows * dm + rows + depth)
            if first < end:
                out.append((dm, first, end))
        return out

    def pack(self, lane, c, fetch):
        edges = ((lane >= 32) & (lane < 40)) | ((lane >= 88) & (lane < 96))
        slot_right = lane // 16
        slot_left = lax.rem(lane + 56, LANES) // 16
        for b in range(self.g.n // SLOT):
            lefts = rights = None
            for s in range(SLOT):
                r = b * SLOT + s
                even, odd, merged = fetch(r)
                self.rm[c, self.base + r] = merged
                both = jnp.where(edges, even, pltpu.roll(odd, 8, 1))
                a = pltpu.roll(both, (16 * s + 40) % LANES, 1)
                z = pltpu.roll(both, (16 * s - 88) % LANES, 1)
                lefts = a if s == 0 else jnp.where(slot_left == s, a, lefts)
                rights = z if s == 0 else jnp.where(slot_right == s, z, rights)
            self.to_left[c, b] = lefts
            self.to_right[c, b] = rights

    def send(self, net):
        n, base = self.g.n, self.base
        for dm, first, end in self.plan(n, self.depth):
            start = base + first - n * dm
            if dm:
                net.send(
                    self.rm.at[:, pl.ds(base + first, end - first)],
                    self.rm.at[:, pl.ds(start, end - first)],
                    0,
                    dm,
                    self.copies,
                )
            low, high = first // SLOT, -(-end // SLOT)
            there = base // SLOT + low - n // SLOT * dm
            for dp, mine, theirs in ((-1, self.to_left, self.right), (1, self.to_right, self.left)):
                net.send(
                    mine.at[:, pl.ds(low, high - low)],
                    theirs.at[:, pl.ds(there, high - low)],
                    dp,
                    dm,
                    self.copies,
                )

    def finish(self, lane, c, own, put):
        inner = (lane >= 32) & (lane < 96)
        for r in range(-self.depth, self.g.n + self.depth):
            block, s = (r + self.base) // SLOT, (r + self.base) % SLOT
            mine = (lane >= 16 * s) & (lane < 16 * s + 16)
            outer = jnp.where(mine, self.left[c, block], self.right[c, block])
            kept = own is not None and 0 <= r < self.g.n
            row = None if kept else self.rm[c, r + self.base]
            for q in range(2):
                value = own(q, r) if kept else pltpu.roll(row, 96 if q else 32, 1)
                margin = pltpu.roll(outer, (24 - 8 * q - 16 * s) % LANES, 1)
                put(q, r, jnp.where(inner, value, margin))


class Net:
    def __init__(self, sems_out, sems_in):
        self.out, self.into, self.count, self.all = sems_out, sems_in, 0, []
        self.p, self.m = lax.axis_index("pre"), lax.axis_index("main")
        self.np, self.nm = lax.axis_size("pre"), lax.axis_size("main")

    def device(self, dp, dm):
        return (lax.rem(self.p + dp + self.np, self.np), lax.rem(self.m + dm + self.nm, self.nm))

    def send(self, src, dst, dp, dm, copies):
        copy = pltpu.make_async_remote_copy(
            src_ref=src,
            dst_ref=dst,
            send_sem=self.out.at[self.count],
            recv_sem=self.into.at[self.count],
            device_id=self.device(dp, dm),
            device_id_type=MESH,
        )
        self.count += 1
        copy.start()
        copies.append(copy)
        self.all.append(copy)


PRE_ROWS, DECK_ROWS = 8, 16
DEPTHS = (12, 11, 10, 9)
DEPTH = DEPTHS[0]
ROWS_IN = DECK_ROWS + 2 * 16
WINDOW = 24
FIRST = -7
NEAR_LOW = -(NEAR // 2) + (FIRST // BLOCK)
NEAR_HIGH = NEAR // 2 - 1 + (FIRST + BLOCK - 1 + WINDOW - 1) // BLOCK


def neighbours_of_all(far):
    out = set()
    for rows in (PRE_ROWS, DECK_ROWS):
        for dm, _, _ in Halo.plan(rows, DEPTH):
            out |= {(dp, dm) for dp in (-1, 0, 1)}
    out |= {(0, d) for d in range(NEAR_LOW, NEAR_HIGH + 1)}
    out |= {(0, -d) for d in range(NEAR_LOW, NEAR_HIGH + 1)}
    out |= {(0, NEAR * h) for h in range(-(far // 2) + 1, far // 2 + 1)}
    out.discard((0, 0))
    return sorted(out)


def kernel(far, pre_hbm, deck_hbm, force_hbm, offsets, weights, shifts, phases, pre_out, deck_out, *scratch):
    scratch = list(scratch)

    def take(count):
        got = scratch[:count]
        del scratch[:count]
        return got

    sems_out, sems_in = take(2)
    pre = Grid(PRE_ROWS, DEPTH, True, take(5))
    deck = Grid(DECK_ROWS, DEPTH, False, take(5))
    pre_halos = [Halo(pre, 1 if t else 3, d, take(5)) for t, d in enumerate((DEPTH,) + DEPTHS[:-1])]
    deck_halos = [Halo(deck, 1 if t else 4, d, take(5)) for t, d in enumerate((DEPTH,) + DEPTHS[:-1])]
    taps, mix = take(2)
    planes = [take(7) for _ in range(STEPS)]
    pre_flat, deck_flat, force_flat = take(3)
    pre_in, deck_in, force_in, sems_load = take(4)

    net = Net(sems_out, sems_in)
    barrier = pltpu.get_barrier_semaphore()
    peers = neighbours_of_all(far)
    for dp, dm in peers:
        pl.semaphore_signal(barrier, inc=1, device_id=net.device(dp, dm), device_id_type=MESH)

    loads = []
    for k, (hbm, here) in enumerate(((pre_hbm, pre_in), (deck_hbm, deck_in), (force_hbm, force_in))):
        loads.append(pltpu.make_async_copy(hbm, here, sems_load.at[k]))
        loads[k].start()

    lane = lax.broadcasted_iota(jnp.int32, (X, LANES), 1)
    masks = []
    for q in range(2):
        place = net.p * LANES + (lane - 32) * 2 + q
        masks.append(jnp.where((place >= 0) & (place < net.np * LANES), 1.0, 0.0))

    z_of = lax.broadcasted_iota(jnp.int32, (LANES, LANES), 0)
    l_of = lax.broadcasted_iota(jnp.int32, (LANES, LANES), 1)
    sort = jnp.where(z_of == jnp.where(l_of < 64, 2 * l_of, 2 * l_of - 127), 1.0, 0.0)
    unsort = jnp.where(l_of == jnp.where(z_of < 64, 2 * z_of, 2 * z_of - 127), 1.0, 0.0)

    def dot(a, b):
        return jnp.dot(a, b, precision=lax.Precision.HIGHEST, preferred_element_type=jnp.float32)

    def load(halo, source, flat, comps, first):
        n = halo.g.n
        for c in range(comps):
            flat[c] = dot(source[pl.ds(c * X * n, X * n)], sort)

            def fetch(r):
                value = flat[c, pl.ds(r, X, stride=n)]
                return pltpu.roll(value, 32, 1), pltpu.roll(value, 96, 1), value

            halo.pack(lane, first + c, fetch)

    def unload(halo, comps):
        g = halo.g

        def one(c, carry):
            def put(q, r, value):
                value = value * masks[q]
                g.put(g.u, value, c, q, g.base + r)
                g.put_high(g.u, value, c, q, g.base + r)

            halo.finish(lane, c, None, put)
            return carry

        lax.fori_loop(0, comps, one, 0)

    def merge(even, odd, at=lane):
        return jnp.where(at < 64, pltpu.roll(even, 96, 1), pltpu.roll(odd, 32, 1))

    def give_pressure(halo):
        g = halo.g

        def fetch(r):
            even, odd = g.at(g.pa, 0, g.base + r), g.at(g.pa, 1, g.base + r)
            return even, odd, merge(even, odd)

        halo.pack(lane, 0, fetch)
        halo.send(net)

    def take_pressure(halo):
        g = halo.g
        for copy in halo.copies:
            copy.wait_recv()

        def put(q, r, value):
            g.put(g.pa, value * masks[q], q, g.base + r)

        halo.finish(lane, 0, lambda q, r: g.at(g.pa, q, g.base + r), put)
        correct(g, halo.depth - 1, masks)

    loads[0].wait()
    load(pre_halos[0], pre_in, pre_flat, 3, 0)
    pl.semaphore_wait(barrier, len(peers))
    pre_halos[0].send(net)
    loads[1].wait()
    loads[2].wait()
    load(deck_halos[0], deck_in, deck_flat, 3, 0)
    load(deck_halos[0], force_in, force_flat, 1, 3)
    deck_halos[0].send(net)
    tap_copies = []
    own_taps = jnp.zeros((DECK_ROWS, LANES), jnp.float32)
    for k in range(TAPS):
        hit = offsets[:, k : k + 1] + 1 == lane
        own_taps = own_taps + jnp.where(hit, weights[:, k : k + 1], 0.0)
    taps[pl.ds(16, DECK_ROWS)] = own_taps
    for dm in (1, -1):
        net.send(taps.at[pl.ds(16, 16)], taps.at[pl.ds(16 - 16 * dm, 16)], 0, dm, tap_copies)
    for ref in (deck.pa, deck.pb):
        ref[:, :, 0:8] = jnp.zeros(ref.shape[:2] + (8, LANES), jnp.float32)
        ref[:, :, 24:32] = jnp.zeros(ref.shape[:2] + (8, LANES), jnp.float32)

    def pre_force(value, c, q, r):
        return value + TIME_STEP * DRIVE if c == 0 else value

    def precursor_step(t):
        if t == 0:
            for copy in pre_halos[0].copies:
                copy.wait_recv()
            unload(pre_halos[0], 3)
        else:
            take_pressure(pre_halos[t])
        solve(pre, DEPTHS[t], 1, masks, pre_force)
        if t + 1 < STEPS:
            give_pressure(pre_halos[t + 1])
        correct(pre, 0, masks)
        block, hop = planes[t][:2]
        wide = lane[:BLOCK]
        for c in range(3):
            for r in range(BLOCK):
                both = [pre.u[c, q, pre.base + r, X - 1 : X] for q in range(2)]
                block[c, r : r + 1] = merge(both[0], both[1], lane[:1])
        hop[0] = block[...]
        copies = []
        for h in range(1, far):
            back = -NEAR * h if h <= far // 2 else NEAR * (far - h)
            net.send(block, hop.at[h], 0, back, copies)
        return copies

    def shift_of(t):
        total = BLOCK * net.nm
        moved = lax.rem(shifts[t] + BLOCK * NEAR // 2, total)
        turn = moved // (BLOCK * NEAR)
        return turn, moved - turn * (BLOCK * NEAR) - BLOCK * NEAR // 2

    def near_hop(t, copies):
        hop, near = planes[t][1:3]
        for copy in copies:
            copy.wait_recv()
        turn, _ = shift_of(t)
        mine = pl.ds(-NEAR_LOW * BLOCK, BLOCK)
        near[:, mine] = hop[turn]
        out = []
        for d in range(NEAR_LOW, NEAR_HIGH + 1):
            if d:
                net.send(near.at[:, mine], near.at[:, pl.ds((d - NEAR_LOW) * BLOCK, BLOCK)], 0, -d, out)
        return out

    def make_mix():
        for copy in tap_copies:
            copy.wait_recv()
        row = lax.broadcasted_iota(jnp.int32, (ROWS_IN, LANES), 0)
        col = lax.broadcasted_iota(jnp.int32, (ROWS_IN, LANES), 1)
        ahead = col - (row // 2 - 8 - 1 - FIRST)
        parts = taps[...]
        total = jnp.zeros((ROWS_IN, LANES), jnp.float32)
        for d in range(4):
            total = jnp.where(ahead == d, parts[:, d : d + 1], total)
        mix[...] = total

    tall = lax.broadcasted_iota(jnp.int32, (ROWS_IN, LANES), 1)

    def inlet(t, copies):
        _, _, near, held, edges, from_left, from_right = planes[t]
        for copy in copies:
            copy.wait_recv()
        _, rest = shift_of(t)
        origin = rest + (FIRST - NEAR_LOW * BLOCK)
        left = right = jnp.zeros((ROWS_IN, LANES), jnp.float32)
        mixing = mix[...][:, :WINDOW]
        for c in range(3):
            value = dot(mixing, near[c, pl.ds(origin, WINDOW)])
            held[c] = value
            low = (tall >= 16 * c) & (tall < 16 * c + 8)
            high = (tall >= 16 * c + 8) & (tall < 16 * c + 16)
            left = jnp.where(low, pltpu.roll(value, 16 * c, 1), left)
            left = jnp.where(high, pltpu.roll(value, (16 * c + 8 - 64) % LANES, 1), left)
            right = jnp.where(low, pltpu.roll(value, (16 * c - 56) % LANES, 1), right)
            right = jnp.where(high, pltpu.roll(value, (16 * c + 8 - 120) % LANES, 1), right)
        edges[0] = left
        edges[1] = right
        out = []
        net.send(edges.at[0], from_right, -1, 0, out)
        net.send(edges.at[1], from_left, 1, 0, out)
        return out

    def ghosts(t, copies):
        _, _, _, held, _, from_left, from_right = planes[t]
        for copy in copies:
            copy.wait_recv()
        depth = DEPTHS[t] - 1
        inner = (tall >= 32) & (tall < 96)
        for q in range(2):
            spots = net.p * LANES + (tall - 32) * 2 + q
            inside = jnp.where((spots >= 0) & (spots < net.np * LANES), 1.0, 0.0)
            for c in range(3):
                value = pltpu.roll(held[c], 96 if q else 32, 1)
                low = pltpu.roll(from_left[...], (24 - 16 * c - 8 * q) % LANES, 1)
                high = pltpu.roll(from_right[...], (96 - 16 * c - 8 * q) % LANES, 1)
                value = jnp.where(inner, value, jnp.where(tall < 64, low, high)) * inside
                for r in range(-depth, DECK_ROWS + depth):
                    line = value[r + 16 : r + 17]
                    deck.u[c, q, deck.base + r, 7:8] = line
                    if c == 0:
                        deck.v[c, q, deck.base + r, 7:8] = line

    def deck_step(t, copies):
        angle = TWO_PI * phases[t].astype(jnp.float32) / PERIOD
        gain = TIME_STEP * FORCING * jnp.sin(jnp.full((X, LANES), angle, jnp.float32))

        def deck_force(value, c, q, r):
            return value + gain * deck.at(deck.u, 3, q, r) if c == 2 else value

        ghosts(t, copies)
        last = t + 1 == STEPS

        def middle():
            near_copies[t + 1] = near_hop(t + 1, far_copies[t + 1])

        solve(deck, DEPTHS[t], 1 if last else 0, masks, deck_force, None if last else middle)
        if last:
            correct(deck, 0, masks)
        else:
            give_pressure(deck_halos[t + 1])

    far_copies = {0: precursor_step(0)}
    for copy in deck_halos[0].copies:
        copy.wait_recv()
    unload(deck_halos[0], 4)
    make_mix()
    near_copies = {0: near_hop(0, far_copies[0])}
    far_copies[1] = precursor_step(1)
    for t in range(STEPS):
        edge_copies = inlet(t, near_copies[t])
        if t:
            take_pressure(deck_halos[t])
        deck_step(t, edge_copies)
        if t + 2 < STEPS:
            far_copies[t + 2] = precursor_step(t + 2)

    def store(g, flat, target):
        for c in range(3):
            for r in range(g.n):
                even, odd = g.at(g.u, c, 0, g.base + r), g.at(g.u, c, 1, g.base + r)
                flat[c, pl.ds(r, X, stride=g.n)] = merge(even, odd)
            target[pl.ds(c * X * g.n, X * g.n)] = dot(flat[c], unsort)

    store(pre, pre_flat, pre_out)
    store(deck, deck_flat, deck_out)
    for copy in net.all:
        copy.wait_send()


def message_count(far):
    count = 0
    for rows in (PRE_ROWS, DECK_ROWS):
        for depth in (DEPTH,) + DEPTHS[:-1]:
            count += 3 * len(Halo.plan(rows, depth))
    return count + 2 + STEPS * (far - 1 + NEAR_HIGH - NEAR_LOW + 2)


def shards(pre_velocity, deck_velocity, deck_force, inlet_shift, tap_offset, tap_weight, phase_index):
    far = lax.axis_size("main") // NEAR
    vmem = pl.BlockSpec(memory_space=pltpu.VMEM)
    smem = pl.BlockSpec(memory_space=pltpu.SMEM)
    hbm = pl.BlockSpec(memory_space=pl.ANY)
    messages = message_count(far)
    scratch = [pltpu.SemaphoreType.DMA((messages,)), pltpu.SemaphoreType.DMA((messages,))]
    scratch += Grid.scratch(PRE_ROWS, DEPTH, True, 3)
    scratch += Grid.scratch(DECK_ROWS, DEPTH, False, 4)
    for t, depth in enumerate((DEPTH,) + DEPTHS[:-1]):
        scratch += Halo.scratch(PRE_ROWS, depth, 1 if t else 3)
    for t, depth in enumerate((DEPTH,) + DEPTHS[:-1]):
        scratch += Halo.scratch(DECK_ROWS, depth, 1 if t else 4)
    scratch += [pltpu.VMEM((ROWS_IN, LANES), jnp.float32)] * 2
    for _ in range(STEPS):
        scratch.append(pltpu.VMEM((3, BLOCK, LANES), jnp.float32))
        scratch.append(pltpu.VMEM((far, 3, BLOCK, LANES), jnp.float32))
        scratch.append(pltpu.VMEM((3, (NEAR_HIGH - NEAR_LOW + 1) * BLOCK, LANES), jnp.float32))
        scratch.append(pltpu.VMEM((3, ROWS_IN, LANES), jnp.float32))
        scratch.append(pltpu.VMEM((2, ROWS_IN, LANES), jnp.float32))
        scratch += [pltpu.VMEM((ROWS_IN, LANES), jnp.float32)] * 2
    scratch.append(pltpu.VMEM((3, X * PRE_ROWS, LANES), jnp.float32))
    scratch.append(pltpu.VMEM((3, X * DECK_ROWS, LANES), jnp.float32))
    scratch.append(pltpu.VMEM((1, X * DECK_ROWS, LANES), jnp.float32))
    for rows in (3 * X * PRE_ROWS, 3 * X * DECK_ROWS, X * DECK_ROWS):
        scratch.append(pltpu.VMEM((rows, LANES), jnp.float32))
    scratch.append(pltpu.SemaphoreType.DMA((3,)))

    pre_rows, deck_rows = 3 * X * PRE_ROWS, 3 * X * DECK_ROWS
    pre, deck = pl.pallas_call(
        functools.partial(kernel, far),
        out_shape=(
            jax.ShapeDtypeStruct((pre_rows, LANES), jnp.float32),
            jax.ShapeDtypeStruct((deck_rows, LANES), jnp.float32),
        ),
        in_specs=[hbm, hbm, hbm, vmem, vmem, smem, smem],
        out_specs=(vmem, vmem),
        scratch_shapes=scratch,
        compiler_params=pltpu.CompilerParams(
            collective_id=0, has_side_effects=True, vmem_limit_bytes=56 * 1024 * 1024
        ),
    )(
        pre_velocity.reshape(pre_rows, LANES),
        deck_velocity.reshape(deck_rows, LANES),
        deck_force.reshape(X * DECK_ROWS, LANES),
        tap_offset,
        tap_weight,
        inlet_shift,
        phase_index,
    )
    return pre.reshape(pre_velocity.shape), deck.reshape(deck_velocity.shape)


def solution(mesh):
    placed = (
        P(None, None, "main", "pre"),
        P(None, None, "main", "pre"),
        P(None, "main", "pre"),
        P(),
        P("main", None),
        P("main", None),
        P(),
    )
    return jax.shard_map(
        shards,
        mesh=mesh,
        in_specs=placed,
        out_specs=(P(None, None, "main", "pre"), P(None, None, "main", "pre")),
        check_vma=False,
    )
```
